32 devices in a mesh: dp: 8 (over z, y), ctx: 4 (over x, core).
Axes of the slice: x: 2, y: 2, z: 4, core: 2. Of those that a mesh axis runs over, the one named last changes fastest.
Arguments:
- queries: bfloat16 [8, 512, 4096], P('dp', 'ctx'), may hold values from -160 to 160
- keys: bfloat16 [8, 512, 512], P('dp', 'ctx'), may hold values from -6 to 6
- values: bfloat16 [8, 512, 512], P('dp', 'ctx'), may hold values from -6 to 6
- doc_start: int32 [8, 512], P('dp', 'ctx'), may hold values from -256 to 511, as said below
Outputs:
- attended: bfloat16 [8, 512, 4096], P('dp', 'ctx')
The draws below stay inside these ranges and needn't reach their ends.
Inputs may be any that keep to these rules, and one draw needn't show every extreme that they name: A document that begins before its slab does so in the slab before, at place -256 or later; in slab 0 every document begins at 0 or later. doc_start never decreases along sequence places, and each token's document begins at or before the token.
All inputs are finite; a program needn't handle non-finite values.
Results may differ from the reference program's by a relative error of at most 0.0035.
Values may be sent and summed in bfloat16 or wider, within the bound.
A program may use at most 64 MiB of HBM per device.

```python
import jax
import jax.numpy as jnp
from jax import lax

H = 32
KVH = 4
HD = 128
TOK_DEV = 128
SLAB_LEN = 512
SLABS = 8
N_CTX = 4


def key_field(key):
    base_field = jax.random.normal(jax.random.fold_in(key, 11), (SLABS, SLAB_LEN, KVH * HD), jnp.float32)
    return jnp.clip(base_field, -6.0, 6.0)


def draw_keys(key, part):
    return key_field(key).astype(jnp.bfloat16)


def draw_queries(key, part):
    base_field = jnp.clip(jax.random.normal(jax.random.fold_in(key, 21), (SLABS, SLAB_LEN, H * HD), jnp.float32), -6.0, 6.0)
    return base_field.astype(jnp.bfloat16)


def draw_doc_start(key, part):
    half_rows = SLAB_LEN // 2
    tok_rows = TOK_DEV
    ctx_count = SLAB_LEN // TOK_DEV
    row_index = jnp.arange(SLAB_LEN, dtype=jnp.int32)
    slab_index = jnp.arange(SLABS, dtype=jnp.int32)[:, None]
    special = jax.random.randint(jax.random.fold_in(key, 33), (), 0, SLABS - 1)
    spare_slab = jax.random.randint(jax.random.fold_in(key, 34), (), 1, SLABS)
    quiet_slab = (slab_index == special + 1) | (slab_index == spare_slab)
    early = jax.random.randint(jax.random.fold_in(key, 31), (SLABS, SLAB_LEN), 0, 24) == 0
    early = early & (row_index[None, :] < half_rows) & (row_index[None, :] > 0)
    early = early & jnp.logical_not(quiet_slab)
    later = half_rows + jax.random.randint(jax.random.fold_in(key, 32), (SLABS, 1), 0, half_rows)
    later = jnp.where(slab_index == special, half_rows, later)
    later = jnp.where(slab_index == special + 1, SLAB_LEN - 1, later)
    flags = early | (row_index[None, :] == later) | (slab_index == 0) & (row_index[None, :] == 0)
    global_pos = slab_index * SLAB_LEN + row_index[None, :]
    marked = jnp.where(flags, global_pos, 0).reshape(-1)
    begins = lax.cummax(marked, axis=0).reshape(SLABS, SLAB_LEN)
    relative = begins - slab_index * SLAB_LEN
    owner = row_index // tok_rows
    row_in = row_index % tok_rows
    half_block = tok_rows // 2
    logical = jnp.where(row_in < half_block, owner, 2 * ctx_count - 1 - owner) * half_block + row_in % half_block
    return relative[:, logical].astype(jnp.int32)


def level_of(own_key, shape, cuts, least, top_value):
    gain = 1.0
    for dim, blocks in cuts:
        steps = jax.random.uniform(jax.random.fold_in(jax.random.fold_in(own_key, 6), dim), (blocks,), jnp.float32, least / len(cuts), top_value / len(cuts))
        gain = gain * jnp.repeat(jnp.exp(steps), shape[dim] // blocks).reshape((-1,) + (1,) * (len(shape) - 1 - dim))
    return gain


def gaussian(key, dims, spread, limit, split=(), kind=jnp.bfloat16):
    values = spread * jax.random.normal(key, dims, jnp.float32)
    if split:
        values = values * level_of(key, dims, split, -0.22, 0.18)
    return jnp.clip(values, -limit, limit).astype(kind)


def setup_inputs(seed: int = 0) -> dict:
    seeds = jax.random.split(jax.random.key(seed), 5)
    queries = draw_queries(jax.random.fold_in(seeds[4], 71), 0)
    keys = draw_keys(jax.random.fold_in(seeds[4], 71), 0)
    values = gaussian(seeds[2], (SLABS, SLAB_LEN, KVH * HD), 1.0, 6.0, ((0, 8), (1, 4)))
    doc_start = draw_doc_start(jax.random.fold_in(seeds[4], 71), 0)
    return dict(queries=queries, keys=keys, values=values, doc_start=doc_start)


ROPE_BASE = 500000.0
NEG_FILL = -1e30


def rotate(field, rel_pos, head_count, head_width):
    half_width = head_width // 2
    inv_freq = ROPE_BASE ** (-2.0 * jnp.arange(half_width, dtype=jnp.float32) / head_width)
    angles = rel_pos.astype(jnp.float32)[:, None] * inv_freq[None, :]
    cosine = jnp.cos(angles)[:, None, :]
    sine = jnp.sin(angles)[:, None, :]
    shaped = field.astype(jnp.float32).reshape(field.shape[0], head_count, head_width)
    first_half = shaped[..., :half_width]
    second_half = shaped[..., half_width:]
    result = jnp.concatenate([first_half * cosine - second_half * sine, second_half * cosine + first_half * sine], axis=-1)
    return result.reshape(field.shape[0], head_count * head_width).astype(jnp.bfloat16)


def reference(queries, keys, values, doc_start):
    half_rows = TOK_DEV // 2
    groups = H // KVH
    score_scale = HD ** -0.5
    row_index = jnp.arange(SLAB_LEN, dtype=jnp.int32)
    owner = row_index // TOK_DEV
    row_in = row_index % TOK_DEV
    stretch_index = jnp.where(row_in < half_rows, owner, 2 * N_CTX - 1 - owner)
    positions = stretch_index * half_rows + row_in % half_rows
    tail_index = (jnp.arange(N_CTX, dtype=jnp.int32)[:, None] * TOK_DEV + half_rows + jnp.arange(half_rows, dtype=jnp.int32)[None, :]).reshape(-1)
    tail_pos = positions[tail_index] - SLAB_LEN
    key_pos = jnp.concatenate([positions, tail_pos])

    def one_slab(slab):
        before = jnp.maximum(slab - 1, 0)
        starts = doc_start[slab]
        prev_starts = doc_start[before][tail_index]
        q_rot = rotate(queries[slab], positions - starts, H, HD)
        k_rot = rotate(keys[slab], positions - starts, KVH, HD)
        k_prev = rotate(keys[before][tail_index], positions[tail_index] - prev_starts, KVH, HD)
        k_all = jnp.concatenate([k_rot, k_prev], axis=0)
        v_all = jnp.concatenate([values[slab], values[before][tail_index]], axis=0)
        allowed = (key_pos[None, :] <= positions[:, None]) & (key_pos[None, :] >= starts[:, None])
        q_heads = q_rot.astype(jnp.float32).reshape(SLAB_LEN, KVH, groups, HD).transpose(1, 2, 0, 3)
        k_heads = k_all.astype(jnp.float32).reshape(-1, KVH, HD).transpose(1, 0, 2)
        v_heads = v_all.astype(jnp.float32).reshape(-1, KVH, HD).transpose(1, 0, 2)

        def one_head(operands):
            q_group, k_group, v_group = operands
            scores = jnp.einsum("gqd,nd->gqn", q_group, k_group, precision=lax.Precision.HIGHEST) * score_scale
            scores = jnp.where(allowed[None], scores, NEG_FILL)
            top_score = jnp.max(scores, axis=-1, keepdims=True)
            weights = jnp.where(allowed[None], jnp.exp(scores - top_score), 0.0)
            total = jnp.sum(weights, axis=-1, keepdims=True)
            return jnp.einsum("gqn,nd->gqd", weights, v_group, precision=lax.Precision.HIGHEST) / total

        mixed = lax.map(one_head, (q_heads, k_heads, v_heads))
        return mixed.transpose(2, 0, 1, 3).reshape(SLAB_LEN, H * HD).astype(jnp.bfloat16)

    return lax.map(one_slab, jnp.arange(queries.shape[0], dtype=jnp.int32))
```

```python
import functools
import math

import jax
import jax.numpy as jnp
import numpy as np
from jax import lax
from jax.experimental import pallas as pl
from jax.experimental.pallas import tpu as pltpu
from jax.sharding import PartitionSpec as P

H = 32
KVH = 4
HD = 128
ROPE_BASE = 500000.0
FILL = -1e30
MESH = pl.DeviceIdType.MESH
C2 = HD ** (-0.5) * math.log2(math.e)


def cos_sin(angles, want_cos):
    n = jnp.floor(angles * (2.0 / math.pi) + 0.5)
    r = ((angles - n * 1.5703125) - n * 4.837512969970703125e-4) - n * 7.54978995489188216e-8
    z = r * r
    s = ((-1.9515295891e-4 * z + 8.3321608736e-3) * z - 1.6666654611e-1) * z * r + r
    c = ((2.443315711809948e-5 * z - 1.388731625493765e-3) * z + 4.166664568298827e-2) * z * z - 0.5 * z + 1.0
    quadrant = n.astype(jnp.int32) + jnp.where(want_cos, 1, 0)
    v = jnp.where((quadrant & 1) == 1, c, s)
    return jnp.where((quadrant & 2) == 2, -v, v)


def kernel(n_ctx, n_dp, q_hbm, k_hbm, v_hbm, ds_hbm, freq_hbm, o_hbm,
           q_in, k_in, ds_in, freq_in, kv, q_rot, bias, m_st, acc, o_buf,
           in_sem, out_sem, recv_sem, fwd_sem, lo_sem, hi_sem, ca_sem, dp_sem):
    N = n_ctx
    d = lax.axis_index("dp")
    c = lax.axis_index("ctx")
    sib = c + 1 - 2 * (c % 2)
    half = q_in.shape[0] // 2
    feats = KVH * HD
    groups = H // KVH
    peers = [lax.rem(c + 2 * t, N) for t in range(1, N // 2)]
    slot_lo = N + c
    slot_hi = 3 * N - 1 - c
    slot_ca = N - 1 - c

    cp_ds = pltpu.make_async_copy(ds_hbm, ds_in, in_sem.at[0])
    cp_fr = pltpu.make_async_copy(freq_hbm, freq_in, in_sem.at[1])
    cp_k = pltpu.make_async_copy(k_hbm.at[0], k_in, in_sem.at[2])
    cp_v0 = pltpu.make_async_copy(v_hbm.at[0, pl.ds(0, half)], kv.at[slot_lo, :, pl.ds(feats, feats)], in_sem.at[3])
    cp_v1 = pltpu.make_async_copy(v_hbm.at[0, pl.ds(half, half)], kv.at[slot_hi, :, pl.ds(feats, feats)], in_sem.at[4])
    cp_q = pltpu.make_async_copy(q_hbm.at[0], q_in, in_sem.at[5])
    for cp in (cp_ds, cp_fr, cp_k, cp_v0, cp_v1, cp_q):
        cp.start()

    barrier = pltpu.get_barrier_semaphore()
    pl.semaphore_signal(barrier, inc=1, device_id=(d, sib), device_id_type=MESH)
    for p in peers:
        pl.semaphore_signal(barrier, inc=1, device_id=(d, p), device_id_type=MESH)

    @pl.when(d > 0)
    def _():
        pl.semaphore_signal(barrier, inc=1, device_id=(d - 1, c), device_id_type=MESH)

    cp_ds.wait()
    cp_fr.wait()
    tok = 2 * half
    starts = jnp.transpose(jnp.broadcast_to(ds_in[...].astype(jnp.float32), (HD, tok)))
    row = lax.broadcasted_iota(jnp.int32, (tok, HD), 0)
    lane = lax.broadcasted_iota(jnp.int32, (tok, HD), 1)
    pos = jnp.where(row < half, c * half + row, (2 * N - 2 - c) * half + row)
    posf = pos.astype(jnp.float32)
    low_lane = lane < HD // 2
    trig = cos_sin((posf - starts) * freq_in[...], low_lane)
    trig_r = pltpu.roll(trig, HD // 2, 1)
    cosine = jnp.where(low_lane, trig, trig_r)
    sine = jnp.where(low_lane, -trig_r, trig)

    cp_k.wait()
    for h in range(KVH):
        x = k_in[:, h * HD:(h + 1) * HD].astype(jnp.float32)
        y = (x * cosine + pltpu.roll(x, HD // 2, 1) * sine).astype(jnp.bfloat16)
        kv[slot_lo, :, h * HD:(h + 1) * HD] = y[:half]
        kv[slot_hi, :, h * HD:(h + 1) * HD] = y[half:]
    cp_v0.wait()
    cp_v1.wait()

    has_next = jnp.where(d < n_dp - 1, 1, 0)
    pl.semaphore_wait(barrier, N // 2 + has_next)

    def push(src_slot, dst_slot, send, dev):
        return pltpu.make_async_remote_copy(
            src_ref=kv.at[src_slot], dst_ref=kv.at[dst_slot], send_sem=send,
            recv_sem=recv_sem.at[dst_slot], device_id=dev, device_id_type=MESH)

    def got(slot):
        push(slot, slot, fwd_sem.at[slot], (d, sib)).wait_recv()

    def forward(slot):
        push(slot, slot, fwd_sem.at[slot], (d, sib)).start()

    to_dp = push(slot_hi, slot_ca, dp_sem.at[0], (d + 1, c))

    @pl.when(d < n_dp - 1)
    def _():
        to_dp.start()

    for t, p in enumerate(peers):
        push(slot_lo, slot_lo, lo_sem.at[t], (d, p)).start()

        @pl.when(p < c)
        def _():
            push(slot_hi, slot_hi, hi_sem.at[t], (d, p)).start()

    forward(slot_lo)

    @pl.when(sib < c)
    def _():
        forward(slot_hi)

    def clear(slot):
        kv[slot] = jnp.zeros(kv.shape[1:], kv.dtype)

    for s in range(2 * N, 3 * N):
        @pl.when(s > slot_hi)
        def _():
            clear(s)

    @pl.when(d == 0)
    def _():
        for s in range(N):
            clear(s)

    for s in range(0, 3 * N * half, 128):
        key = (lane + (s - N * half)).astype(jnp.float32)
        bias[:, s:s + 128] = jnp.where((key <= posf) & (key >= starts), 0.0, FILL)

    cp_q.wait()
    for h in range(H):
        x = q_in[:, h * HD:(h + 1) * HD].astype(jnp.float32)
        y = (x * cosine + pltpu.roll(x, HD // 2, 1) * sine).astype(jnp.bfloat16)
        g = h % groups
        q_rot[h // groups, g * half:(g + 1) * half] = y[:half]
        q_rot[h // groups, (groups + g) * half:(groups + g + 1) * half] = y[half:]

    for p in peers:
        got(N + p)
        forward(N + p)

        @pl.when(p > c)
        def _():
            got(3 * N - 1 - p)
            forward(3 * N - 1 - p)

    @pl.when(d > 0)
    def _():
        got(slot_ca)
        for t, p in enumerate(peers):
            push(slot_ca, slot_ca, ca_sem.at[t], (d, p)).start()
        forward(slot_ca)

    got(N + sib)

    @pl.when(sib > c)
    def _():
        got(3 * N - 1 - sib)
    for p in peers:
        ps = p + 1 - 2 * (p % 2)
        got(N + ps)

        @pl.when(p > c)
        def _():
            got(3 * N - 1 - ps)

    rows = groups * half
    ones = jnp.ones((N * half, HD), jnp.bfloat16)

    def piece(kvh, which, base, first):
        col = pl.multiple_of(kvh * HD, HD)
        vcol = pl.multiple_of(feats + kvh * HD, HD)
        k = kv[base:base + N, :, pl.ds(col, HD)].reshape(N * half, HD)
        v = kv[base:base + N, :, pl.ds(vcol, HD)].reshape(N * half, HD)
        va = jnp.concatenate([v, ones], axis=1)
        for w in which:
            r0 = w * rows
            q = q_rot[kvh, r0:r0 + rows]
            s = lax.dot_general(q, k, (((1,), (1,)), ((), ())), preferred_element_type=jnp.float32)
            b = bias[w * half:(w + 1) * half, base * half:(base + N) * half]
            s = s.reshape(groups, half, N * half) * C2 + b[None]
            top = jnp.max(s, axis=-1, keepdims=True).reshape(rows, 1)
            if not first:
                old = m_st[kvh, r0:r0 + rows]
                new = jnp.maximum(old, top)
                scale = jnp.exp2(old - new)
                top = new[:, :1]
            else:
                new = jnp.broadcast_to(top, (rows, HD))
            m_st[kvh, r0:r0 + rows] = new
            wide = jnp.concatenate([new] * (N * half // HD), axis=1)
            w_bf = jnp.exp2(s.reshape(rows, N * half) - wide).astype(jnp.bfloat16)
            pv = jnp.dot(w_bf, va, preferred_element_type=jnp.float32)
            if not first:
                pv = pv + acc[kvh, r0:r0 + rows] * jnp.concatenate([scale, scale], axis=1)
            acc[kvh, r0:r0 + rows] = pv

    def low_high(kvh, _):
        piece(kvh, (0, 1), N, True)
        piece(kvh, (1,), 2 * N, False)
        return _

    lax.fori_loop(0, KVH, low_high, 0)

    @pl.when(d > 0)
    def _():
        for p in peers:
            got(N - 1 - p)
            forward(N - 1 - p)
        got(N - 1 - sib)
        for p in peers:
            ps = p + 1 - 2 * (p % 2)
            got(N - 1 - ps)

    def carried(kvh, _):
        piece(kvh, (0, 1), 0, False)
        for w in range(2):
            for g in range(groups):
                r0 = w * rows + g * half
                a = acc[kvh, r0:r0 + half]
                o = (a[:, :HD] / a[:, HD:]).astype(jnp.bfloat16)
                o_buf[kvh, w * half:(w + 1) * half, g * HD:(g + 1) * HD] = o
        pltpu.make_async_copy(o_buf.at[kvh], o_hbm.at[0, :, pl.ds(pl.multiple_of(kvh * groups * HD, HD), groups * HD)], out_sem.at[kvh]).start()
        return _

    lax.fori_loop(0, KVH, carried, 0)

    for kvh in range(KVH):
        pltpu.make_async_copy(o_buf.at[kvh], o_hbm.at[0, :, pl.ds(kvh * groups * HD, groups * HD)], out_sem.at[kvh]).wait()

    def sent(slot, sem):
        push(slot, slot, sem, (d, sib)).wait_send()

    for t, p in enumerate(peers):
        sent(slot_lo, lo_sem.at[t])
        sent(N + p, fwd_sem.at[N + p])

        @pl.when(p < c)
        def _():
            sent(slot_hi, hi_sem.at[t])

        @pl.when(p > c)
        def _():
            sent(3 * N - 1 - p, fwd_sem.at[3 * N - 1 - p])

        @pl.when(d > 0)
        def _():
            sent(slot_ca, ca_sem.at[t])
            sent(N - 1 - p, fwd_sem.at[N - 1 - p])
    sent(slot_lo, fwd_sem.at[slot_lo])

    @pl.when(sib < c)
    def _():
        sent(slot_hi, fwd_sem.at[slot_hi])

    @pl.when(d > 0)
    def _():
        sent(slot_ca, fwd_sem.at[slot_ca])

    @pl.when(d < n_dp - 1)
    def _():
        sent(slot_hi, dp_sem.at[0])


def solution(mesh):
    n_ctx = mesh.shape["ctx"]
    n_dp = mesh.shape["dp"]
    freq = ROPE_BASE ** (-2.0 * np.arange(HD // 2, dtype=np.float64) / HD)
    freq = np.concatenate([freq, freq]).astype(np.float32)[None]

    def per_device(queries, keys, values, doc_start):
        tok = queries.shape[1]
        half = tok // 2
        groups = H // KVH
        np_half = max(n_ctx // 2 - 1, 1)
        hbm = pl.BlockSpec(memory_space=pl.ANY)
        return pl.pallas_call(
            functools.partial(kernel, n_ctx, n_dp),
            out_shape=jax.ShapeDtypeStruct(queries.shape, jnp.bfloat16),
            in_specs=[hbm] * 5,
            out_specs=hbm,
            scratch_shapes=[
                pltpu.VMEM((tok, H * HD), jnp.bfloat16),
                pltpu.VMEM((tok, KVH * HD), jnp.bfloat16),
                pltpu.VMEM((1, tok), jnp.int32),
                pltpu.VMEM((1, HD), jnp.float32),
                pltpu.VMEM((3 * n_ctx, half, 2 * KVH * HD), jnp.bfloat16),
                pltpu.VMEM((KVH, groups * tok, HD), jnp.bfloat16),
                pltpu.VMEM((tok, 3 * n_ctx * half), jnp.float32),
                pltpu.VMEM((KVH, groups * tok, HD), jnp.float32),
                pltpu.VMEM((KVH, groups * tok, 2 * HD), jnp.float32),
                pltpu.VMEM((KVH, tok, groups * HD), jnp.bfloat16),
                pltpu.SemaphoreType.DMA((6,)),
                pltpu.SemaphoreType.DMA((KVH,)),
                pltpu.SemaphoreType.DMA((3 * n_ctx,)),
                pltpu.SemaphoreType.DMA((3 * n_ctx,)),
                pltpu.SemaphoreType.DMA((np_half,)),
                pltpu.SemaphoreType.DMA((np_half,)),
                pltpu.SemaphoreType.DMA((np_half,)),
                pltpu.SemaphoreType.DMA((1,)),
            ],
            compiler_params=pltpu.CompilerParams(
                collective_id=0, has_side_effects=True, vmem_limit_bytes=48 * 1024 * 1024
            ),
        )(queries, keys, values, doc_start, jnp.asarray(freq))

    return jax.shard_map(
        per_device,
        mesh=mesh,
        in_specs=(P("dp", "ctx", None), P("dp", "ctx", None), P("dp", "ctx", None), P("dp", "ctx")),
        out_specs=P("dp", "ctx", None),
        check_vma=False,
    )
```

```python
import functools
import math

import jax
import jax.numpy as jnp
import numpy as np
from jax import lax
from jax.experimental import pallas as pl
from jax.experimental.pallas import tpu as pltpu
from jax.sharding import PartitionSpec as P

H = 32
KVH = 4
HD = 128
ROPE_BASE = 500000.0
FILL = -1e30
MESH = pl.DeviceIdType.MESH
C2 = HD ** (-0.5) * math.log2(math.e)


def cos_sin(angles, want_cos):
    n = jnp.floor(angles * (2.0 / math.pi) + 0.5)
    r = ((angles - n * 1.5703125) - n * 4.837512969970703125e-4) - n * 7.54978995489188216e-8
    z = r * r
    s = ((-1.9515295891e-4 * z + 8.3321608736e-3) * z - 1.6666654611e-1) * z * r + r
    c = ((2.443315711809948e-5 * z - 1.388731625493765e-3) * z + 4.166664568298827e-2) * z * z - 0.5 * z + 1.0
    quadrant = n.astype(jnp.int32) + jnp.where(want_cos, 1, 0)
    v = jnp.where((quadrant & 1) == 1, c, s)
    return jnp.where((quadrant & 2) == 2, -v, v)


def kernel(n_ctx, n_dp, q_hbm, k_hbm, v_hbm, ds_hbm, freq_hbm, o_hbm,
           q_in, k_in, ds_in, freq_in, kv, q_rot, bias, m_st, acc, o_buf,
           in_sem, out_sem, recv_sem, fwd_sem, lo_sem, hi_sem, ca_sem, dp_sem):
    N = n_ctx
    d = lax.axis_index("dp")
    c = lax.axis_index("ctx")
    sib = c + 1 - 2 * (c % 2)
    half = q_in.shape[0] // 2
    feats = KVH * HD
    groups = H // KVH
    peers = [lax.rem(c + 2 * t, N) for t in range(1, N // 2)]
    slot_lo = N + c
    slot_hi = 3 * N - 1 - c
    slot_ca = N - 1 - c

    cp_ds = pltpu.make_async_copy(ds_hbm, ds_in, in_sem.at[0])
    cp_fr = pltpu.make_async_copy(freq_hbm, freq_in, in_sem.at[1])
    cp_k = pltpu.make_async_copy(k_hbm.at[0], k_in, in_sem.at[2])
    cp_v0 = pltpu.make_async_copy(v_hbm.at[0, pl.ds(0, half)], kv.at[slot_lo, :, pl.ds(feats, feats)], in_sem.at[3])
    cp_v1 = pltpu.make_async_copy(v_hbm.at[0, pl.ds(half, half)], kv.at[slot_hi, :, pl.ds(feats, feats)], in_sem.at[4])
    cp_q = pltpu.make_async_copy(q_hbm.at[0], q_in, in_sem.at[5])
    for cp in (cp_ds, cp_fr, cp_k, cp_v0, cp_v1, cp_q):
        cp.start()

    barrier = pltpu.get_barrier_semaphore()
    pl.semaphore_signal(barrier, inc=1, device_id=(d, sib), device_id_type=MESH)
    for p in peers:
        pl.semaphore_signal(barrier, inc=1, device_id=(d, p), device_id_type=MESH)

    @pl.when(d > 0)
    def _():
        pl.semaphore_signal(barrier, inc=1, device_id=(d - 1, c), device_id_type=MESH)

    cp_ds.wait()
    cp_fr.wait()
    tok = 2 * half
    starts = jnp.transpose(jnp.broadcast_to(ds_in[...].astype(jnp.float32), (HD, tok)))
    row = lax.broadcasted_iota(jnp.int32, (tok, HD), 0)
    lane = lax.broadcasted_iota(jnp.int32, (tok, HD), 1)
    pos = jnp.where(row < half, c * half + row, (2 * N - 2 - c) * half + row)
    posf = pos.astype(jnp.float32)
    low_lane = lane < HD // 2
    trig = cos_sin((posf - starts) * freq_in[...], low_lane)
    trig_r = pltpu.roll(trig, HD // 2, 1)
    cosine = jnp.where(low_lane, trig, trig_r)
    sine = jnp.where(low_lane, -trig_r, trig)

    cp_k.wait()
    for h in range(KVH):
        x = k_in[:, h * HD:(h + 1) * HD].astype(jnp.float32)
        y = (x * cosine + pltpu.roll(x, HD // 2, 1) * sine).astype(jnp.bfloat16)
        kv[slot_lo, :, h * HD:(h + 1) * HD] = y[:half]
        kv[slot_hi, :, h * HD:(h + 1) * HD] = y[half:]
    cp_v0.wait()
    cp_v1.wait()

    has_next = jnp.where(d < n_dp - 1, 1, 0)
    pl.semaphore_wait(barrier, N // 2 + has_next)

    def push(src_slot, dst_slot, send, dev):
        return pltpu.make_async_remote_copy(
            src_ref=kv.at[src_slot], dst_ref=kv.at[dst_slot], send_sem=send,
            recv_sem=recv_sem.at[dst_slot], device_id=dev, device_id_type=MESH)

    def got(slot):
        push(slot, slot, fwd_sem.at[slot], (d, sib)).wait_recv()

    def forward(slot):
        push(slot, slot, fwd_sem.at[slot], (d, sib)).start()

    to_dp = push(slot_hi, slot_ca, dp_sem.at[0], (d + 1, c))

    @pl.when(d < n_dp - 1)
    def _():
        to_dp.start()

    for t, p in enumerate(peers):
        @pl.when(p < c)
        def _():
            push(slot_hi, slot_hi, hi_sem.at[t], (d, p)).start()

    for t, p in enumerate(peers):
        push(slot_lo, slot_lo, lo_sem.at[t], (d, p)).start()

    forward(slot_lo)

    @pl.when(sib < c)
    def _():
        forward(slot_hi)

    def clear(slot):
        kv[slot] = jnp.zeros(kv.shape[1:], kv.dtype)

    for s in range(2 * N, 3 * N):
        @pl.when(s > slot_hi)
        def _():
            clear(s)

    @pl.when(d == 0)
    def _():
        for s in range(N):
            clear(s)

    for s in range(0, 3 * N * half, 128):
        key = (lane + (s - N * half)).astype(jnp.float32)
        bias[:, s:s + 128] = jnp.where((key <= posf) & (key >= starts), 0.0, FILL)

    cp_q.wait()
    for h in range(H):
        x = q_in[:, h * HD:(h + 1) * HD].astype(jnp.float32)
        y = (x * cosine + pltpu.roll(x, HD // 2, 1) * sine).astype(jnp.bfloat16)
        g = h % groups
        q_rot[h // groups, g * half:(g + 1) * half] = y[:half]
        q_rot[h // groups, (groups + g) * half:(groups + g + 1) * half] = y[half:]

    for t, p in enumerate(peers):
        @pl.when(p > c)
        def _():
            got(3 * N - 1 - p)
            forward(3 * N - 1 - p)

            @pl.when(d < n_dp - 1)
            def _():
                push(3 * N - 1 - p, N - 1 - p, dp_sem.at[1 + t], (d + 1, c)).start()

    @pl.when(d > 0)
    def _():
        got(slot_ca)
        for t, p in enumerate(peers):
            @pl.when(p > c)
            def _():
                push(slot_ca, slot_ca, ca_sem.at[t], (d, p)).start()
        forward(slot_ca)

    for p in peers:
        got(N + p)
        forward(N + p)
    got(N + sib)
    for p in peers:
        got(N + p + 1 - 2 * (p % 2))

    rows = groups * half
    ones = jnp.ones((N * half, HD), jnp.bfloat16)

    def piece(kvh, which, base, first):
        col = pl.multiple_of(kvh * HD, HD)
        vcol = pl.multiple_of(feats + kvh * HD, HD)
        k = kv[base:base + N, :, pl.ds(col, HD)].reshape(N * half, HD)
        v = kv[base:base + N, :, pl.ds(vcol, HD)].reshape(N * half, HD)
        va = jnp.concatenate([v, ones], axis=1)
        for w in which:
            r0 = w * rows
            q = q_rot[kvh, r0:r0 + rows]
            s = lax.dot_general(q, k, (((1,), (1,)), ((), ())), preferred_element_type=jnp.float32)
            b = bias[w * half:(w + 1) * half, base * half:(base + N) * half]
            s = s.reshape(groups, half, N * half) * C2 + b[None]
            top = jnp.max(s, axis=-1, keepdims=True).reshape(rows, 1)
            if not first:
                old = m_st[kvh, r0:r0 + rows]
                new = jnp.maximum(old, top)
                scale = jnp.exp2(old - new)
                top = new[:, :1]
            else:
                new = jnp.broadcast_to(top, (rows, HD))
            m_st[kvh, r0:r0 + rows] = new
            wide = jnp.concatenate([new] * (N * half // HD), axis=1)
            w_bf = jnp.exp2(s.reshape(rows, N * half) - wide).astype(jnp.bfloat16)
            pv = jnp.dot(w_bf, va, preferred_element_type=jnp.float32)
            if not first:
                pv = pv + acc[kvh, r0:r0 + rows] * jnp.concatenate([scale, scale], axis=1)
            acc[kvh, r0:r0 + rows] = pv

    def low(kvh, _):
        piece(kvh, (0, 1), N, True)
        return _

    def high(kvh, _):
        piece(kvh, (1,), 2 * N, False)
        return _

    lax.fori_loop(0, KVH, low, 0)

    @pl.when(d > 0)
    def _():
        for p in peers:
            got(N - 1 - p)
            forward(N - 1 - p)

    @pl.when(sib > c)
    def _():
        got(3 * N - 1 - sib)
    for p in peers:
        @pl.when(p > c)
        def _():
            got(3 * N - 1 - (p + 1 - 2 * (p % 2)))

    lax.fori_loop(0, KVH, high, 0)

    @pl.when(d > 0)
    def _():
        got(N - 1 - sib)
        for p in peers:
            got(N - 1 - (p + 1 - 2 * (p % 2)))

    def carried(kvh, _):
        piece(kvh, (0, 1), 0, False)
        for w in range(2):
            for g in range(groups):
                r0 = w * rows + g * half
                a = acc[kvh, r0:r0 + half]
                o = (a[:, :HD] / a[:, HD:]).astype(jnp.bfloat16)
                o_buf[kvh, w * half:(w + 1) * half, g * HD:(g + 1) * HD] = o
        pltpu.make_async_copy(o_buf.at[kvh], o_hbm.at[0, :, pl.ds(pl.multiple_of(kvh * groups * HD, HD), groups * HD)], out_sem.at[kvh]).start()
        return _

    lax.fori_loop(0, KVH, carried, 0)

    for kvh in range(KVH):
        pltpu.make_async_copy(o_buf.at[kvh], o_hbm.at[0, :, pl.ds(kvh * groups * HD, groups * HD)], out_sem.at[kvh]).wait()

    def sent(slot, sem):
        push(slot, slot, sem, (d, sib)).wait_send()

    for t, p in enumerate(peers):
        sent(slot_lo, lo_sem.at[t])
        sent(N + p, fwd_sem.at[N + p])

        @pl.when(p < c)
        def _():
            sent(slot_hi, hi_sem.at[t])

        @pl.when(p > c)
        def _():
            sent(3 * N - 1 - p, fwd_sem.at[3 * N - 1 - p])

            @pl.when(d < n_dp - 1)
            def _():
                sent(3 * N - 1 - p, dp_sem.at[1 + t])

            @pl.when(d > 0)
            def _():
                sent(slot_ca, ca_sem.at[t])

        @pl.when(d > 0)
        def _():
            sent(N - 1 - p, fwd_sem.at[N - 1 - p])
    sent(slot_lo, fwd_sem.at[slot_lo])

    @pl.when(sib < c)
    def _():
        sent(slot_hi, fwd_sem.at[slot_hi])

    @pl.when(d > 0)
    def _():
        sent(slot_ca, fwd_sem.at[slot_ca])

    @pl.when(d < n_dp - 1)
    def _():
        sent(slot_hi, dp_sem.at[0])


def solution(mesh):
    n_ctx = mesh.shape["ctx"]
    n_dp = mesh.shape["dp"]
    freq = ROPE_BASE ** (-2.0 * np.arange(HD // 2, dtype=np.float64) / HD)
    freq = np.concatenate([freq, freq]).astype(np.float32)[None]

    def per_device(queries, keys, values, doc_start):
        tok = queries.shape[1]
        half = tok // 2
        groups = H // KVH
        np_half = max(n_ctx // 2 - 1, 1)
        hbm = pl.BlockSpec(memory_space=pl.ANY)
        return pl.pallas_call(
            functools.partial(kernel, n_ctx, n_dp),
            out_shape=jax.ShapeDtypeStruct(queries.shape, jnp.bfloat16),
            in_specs=[hbm] * 5,
            out_specs=pl.BlockSpec(memory_space=pl.ANY),
            scratch_shapes=[
                pltpu.VMEM((tok, H * HD), jnp.bfloat16),
                pltpu.VMEM((tok, KVH * HD), jnp.bfloat16),
                pltpu.VMEM((1, tok), jnp.int32),
                pltpu.VMEM((1, HD), jnp.float32),
                pltpu.VMEM((3 * n_ctx, half, 2 * KVH * HD), jnp.bfloat16),
                pltpu.VMEM((KVH, groups * tok, HD), jnp.bfloat16),
                pltpu.VMEM((tok, 3 * n_ctx * half), jnp.float32),
                pltpu.VMEM((KVH, groups * tok, HD), jnp.float32),
                pltpu.VMEM((KVH, groups * tok, 2 * HD), jnp.float32),
                pltpu.VMEM((KVH, tok, groups * HD), jnp.bfloat16),
                pltpu.SemaphoreType.DMA((6,)),
                pltpu.SemaphoreType.DMA((KVH,)),
                pltpu.SemaphoreType.DMA((3 * n_ctx,)),
                pltpu.SemaphoreType.DMA((3 * n_ctx,)),
                pltpu.SemaphoreType.DMA((np_half,)),
                pltpu.SemaphoreType.DMA((np_half,)),
                pltpu.SemaphoreType.DMA((np_half,)),
                pltpu.SemaphoreType.DMA((1 + np_half,)),
            ],
            compiler_params=pltpu.CompilerParams(
                collective_id=0, has_side_effects=True, vmem_limit_bytes=63 * 1024 * 1024
            ),
        )(queries, keys, values, doc_start, jnp.asarray(freq))

    return jax.shard_map(
        per_device,
        mesh=mesh,
        in_specs=(P("dp", "ctx", None), P("dp", "ctx", None), P("dp", "ctx", None), P("dp", "ctx")),
        out_specs=P("dp", "ctx", None),
        check_vma=False,
    )
```

```python
import functools
import math

import jax
import jax.numpy as jnp
import numpy as np
from jax import lax
from jax.experimental import pallas as pl
from jax.experimental.pallas import tpu as pltpu
from jax.sharding import PartitionSpec as P

H = 32
KVH = 4
HD = 128
ROPE_BASE = 500000.0
FILL = -1e30
MESH = pl.DeviceIdType.MESH
C2 = HD ** (-0.5) * math.log2(math.e)


def cos_sin(angles, want_cos):
    n = jnp.floor(angles * (2.0 / math.pi) + 0.5)
    r = ((angles - n * 1.5703125) - n * 4.837512969970703125e-4) - n * 7.54978995489188216e-8
    z = r * r
    s = ((-1.9515295891e-4 * z + 8.3321608736e-3) * z - 1.6666654611e-1) * z * r + r
    c = ((2.443315711809948e-5 * z - 1.388731625493765e-3) * z + 4.166664568298827e-2) * z * z - 0.5 * z + 1.0
    quadrant = n.astype(jnp.int32) + jnp.where(want_cos, 1, 0)
    v = jnp.where((quadrant & 1) == 1, c, s)
    return jnp.where((quadrant & 2) == 2, -v, v)


def kernel(n_ctx, n_dp, q_hbm, k_hbm, v_hbm, ds_hbm, freq_hbm, o_hbm,
           q_in, k_in, ds_in, freq_in, kv, q_rot, bias, m_st, acc, o_buf,
           in_sem, out_sem, recv_sem, fwd_sem, lo_sem, hi_sem, ca_sem, dp_sem):
    N = n_ctx
    d = lax.axis_index("dp")
    c = lax.axis_index("ctx")
    sib = c + 1 - 2 * (c % 2)
    half = q_in.shape[0] // 2
    feats = KVH * HD
    groups = H // KVH
    peers = [lax.rem(c + 2 * t, N) for t in range(1, N // 2)]
    slot_lo = N + c
    slot_hi = 3 * N - 1 - c
    slot_ca = N - 1 - c

    cp_ds = pltpu.make_async_copy(ds_hbm, ds_in, in_sem.at[0])
    cp_fr = pltpu.make_async_copy(freq_hbm, freq_in, in_sem.at[1])
    cp_k = pltpu.make_async_copy(k_hbm.at[0], k_in, in_sem.at[2])
    cp_v0 = pltpu.make_async_copy(v_hbm.at[0, pl.ds(0, half)], kv.at[slot_lo, :, pl.ds(feats, feats)], in_sem.at[3])
    cp_v1 = pltpu.make_async_copy(v_hbm.at[0, pl.ds(half, half)], kv.at[slot_hi, :, pl.ds(feats, feats)], in_sem.at[4])
    cp_q = pltpu.make_async_copy(q_hbm.at[0], q_in, in_sem.at[5])
    for cp in (cp_ds, cp_fr, cp_k, cp_v0, cp_v1, cp_q):
        cp.start()

    barrier = pltpu.get_barrier_semaphore()
    pl.semaphore_signal(barrier, inc=1, device_id=(d, sib), device_id_type=MESH)
    for p in peers:
        pl.semaphore_signal(barrier, inc=1, device_id=(d, p), device_id_type=MESH)

    @pl.when(d > 0)
    def _():
        pl.semaphore_signal(barrier, inc=1, device_id=(d - 1, c), device_id_type=MESH)

    cp_ds.wait()
    cp_fr.wait()
    tok = 2 * half
    starts = jnp.transpose(jnp.broadcast_to(ds_in[...].astype(jnp.float32), (HD, tok)))
    row = lax.broadcasted_iota(jnp.int32, (tok, HD), 0)
    lane = lax.broadcasted_iota(jnp.int32, (tok, HD), 1)
    pos = jnp.where(row < half, c * half + row, (2 * N - 2 - c) * half + row)
    posf = pos.astype(jnp.float32)
    low_lane = lane < HD // 2
    trig = cos_sin((posf - starts) * freq_in[...], low_lane)
    trig_r = pltpu.roll(trig, HD // 2, 1)
    cosine = jnp.where(low_lane, trig, trig_r)
    sine = jnp.where(low_lane, -trig_r, trig)

    cp_k.wait()
    for h in range(KVH):
        x = k_in[:, h * HD:(h + 1) * HD].astype(jnp.float32)
        y = (x * cosine + pltpu.roll(x, HD // 2, 1) * sine).astype(jnp.bfloat16)
        kv[slot_lo, :, h * HD:(h + 1) * HD] = y[:half]
        kv[slot_hi, :, h * HD:(h + 1) * HD] = y[half:]
    cp_v0.wait()
    cp_v1.wait()

    has_next = jnp.where(d < n_dp - 1, 1, 0)
    pl.semaphore_wait(barrier, N // 2 + has_next)

    def push(src_slot, dst_slot, send, dev):
        return pltpu.make_async_remote_copy(
            src_ref=kv.at[src_slot], dst_ref=kv.at[dst_slot], send_sem=send,
            recv_sem=recv_sem.at[dst_slot], device_id=dev, device_id_type=MESH)

    def got(slot):
        push(slot, slot, fwd_sem.at[slot], (d, sib)).wait_recv()

    def forward(slot):
        push(slot, slot, fwd_sem.at[slot], (d, sib)).start()

    to_dp = push(slot_hi, slot_ca, dp_sem.at[0], (d + 1, c))

    @pl.when(d < n_dp - 1)
    def _():
        to_dp.start()

    for t, p in enumerate(peers):
        @pl.when(p < c)
        def _():
            push(slot_hi, slot_hi, hi_sem.at[t], (d, p)).start()

    for t, p in enumerate(peers):
        push(slot_lo, slot_lo, lo_sem.at[t], (d, p)).start()

    forward(slot_lo)

    @pl.when(sib < c)
    def _():
        forward(slot_hi)

    def clear(slot):
        kv[slot] = jnp.zeros(kv.shape[1:], kv.dtype)

    for s in range(2 * N, 3 * N):
        @pl.when(s > slot_hi)
        def _():
            clear(s)

    @pl.when(d == 0)
    def _():
        for s in range(N):
            clear(s)

    for s in range(0, 3 * N * half, 128):
        key = (lane + (s - N * half)).astype(jnp.float32)
        bias[:, s:s + 128] = jnp.where((key <= posf) & (key >= starts), 0.0, FILL)

    cp_q.wait()
    for h in range(H):
        x = q_in[:, h * HD:(h + 1) * HD].astype(jnp.float32)
        y = (x * cosine + pltpu.roll(x, HD // 2, 1) * sine).astype(jnp.bfloat16)
        g = h % groups
        q_rot[h // groups, g * half:(g + 1) * half] = y[:half]
        q_rot[h // groups, (groups + g) * half:(groups + g + 1) * half] = y[half:]

    for t, p in enumerate(peers):
        @pl.when(p > c)
        def _():
            got(3 * N - 1 - p)
            forward(3 * N - 1 - p)

            @pl.when(d < n_dp - 1)
            def _():
                push(3 * N - 1 - p, N - 1 - p, dp_sem.at[1 + t], (d + 1, c)).start()

    @pl.when(d > 0)
    def _():
        got(slot_ca)
        for t, p in enumerate(peers):
            @pl.when(p > c)
            def _():
                push(slot_ca, slot_ca, ca_sem.at[t], (d, p)).start()
        forward(slot_ca)

    for p in peers:
        got(N + p)
        forward(N + p)
    got(N + sib)
    for p in peers:
        got(N + p + 1 - 2 * (p % 2))

    rows = groups * half
    ones = jnp.ones((N * half, HD), jnp.bfloat16)

    def piece(kvh, which, base, first):
        col = pl.multiple_of(kvh * HD, HD)
        vcol = pl.multiple_of(feats + kvh * HD, HD)
        k = kv[base:base + N, :, pl.ds(col, HD)].reshape(N * half, HD)
        v = kv[base:base + N, :, pl.ds(vcol, HD)].reshape(N * half, HD)
        va = jnp.concatenate([v, ones], axis=1)
        for w in which:
            r0 = w * rows
            q = q_rot[kvh, r0:r0 + rows]
            s = lax.dot_general(q, k, (((1,), (1,)), ((), ())), preferred_element_type=jnp.float32)
            b = bias[w * half:(w + 1) * half, base * half:(base + N) * half]
            s = s.reshape(groups, half, N * half) * C2 + b[None]
            top = jnp.max(s, axis=-1, keepdims=True).reshape(rows, 1)
            if not first:
                old = m_st[kvh, r0:r0 + rows]
                new = jnp.maximum(old, top)
                scale = jnp.exp2(old - new)
                top = new[:, :1]
            else:
                new = jnp.broadcast_to(top, (rows, HD))
            m_st[kvh, r0:r0 + rows] = new
            wide = jnp.concatenate([new] * (N * half // HD), axis=1)
            w_bf = jnp.exp2(s.reshape(rows, N * half) - wide).astype(jnp.bfloat16)
            pv = jnp.dot(w_bf, va, preferred_element_type=jnp.float32)
            if not first:
                pv = pv + acc[kvh, r0:r0 + rows] * jnp.concatenate([scale, scale], axis=1)
            acc[kvh, r0:r0 + rows] = pv

    def low(kvh, _):
        piece(kvh, (0, 1), N, True)
        return _

    def high(kvh, _):
        piece(kvh, (1,), 2 * N, False)
        return _

    lax.fori_loop(0, KVH, low, 0, unroll=True)

    @pl.when(d > 0)
    def _():
        for p in peers:
            got(N - 1 - p)
            forward(N - 1 - p)

    @pl.when(sib > c)
    def _():
        got(3 * N - 1 - sib)
    for p in peers:
        @pl.when(p > c)
        def _():
            got(3 * N - 1 - (p + 1 - 2 * (p % 2)))

    lax.fori_loop(0, KVH, high, 0, unroll=True)

    @pl.when(d > 0)
    def _():
        got(N - 1 - sib)
        for p in peers:
            got(N - 1 - (p + 1 - 2 * (p % 2)))

    def carried(kvh, _):
        piece(kvh, (0, 1), 0, False)
        for w in range(2):
            for g in range(groups):
                r0 = w * rows + g * half
                a = acc[kvh, r0:r0 + half]
                o = (a[:, :HD] / a[:, HD:]).astype(jnp.bfloat16)
                o_buf[kvh, w * half:(w + 1) * half, g * HD:(g + 1) * HD] = o
        pltpu.make_async_copy(o_buf.at[kvh], o_hbm.at[0, :, pl.ds(pl.multiple_of(kvh * groups * HD, HD), groups * HD)], out_sem.at[kvh]).start()
        return _

    lax.fori_loop(0, KVH, carried, 0, unroll=True)

    for kvh in range(KVH):
        pltpu.make_async_copy(o_buf.at[kvh], o_hbm.at[0, :, pl.ds(kvh * groups * HD, groups * HD)], out_sem.at[kvh]).wait()

    def sent(slot, sem):
        push(slot, slot, sem, (d, sib)).wait_send()

    for t, p in enumerate(peers):
        sent(slot_lo, lo_sem.at[t])
        sent(N + p, fwd_sem.at[N + p])

        @pl.when(p < c)
        def _():
            sent(slot_hi, hi_sem.at[t])

        @pl.when(p > c)
        def _():
            sent(3 * N - 1 - p, fwd_sem.at[3 * N - 1 - p])

            @pl.when(d < n_dp - 1)
            def _():
                sent(3 * N - 1 - p, dp_sem.at[1 + t])

            @pl.when(d > 0)
            def _():
                sent(slot_ca, ca_sem.at[t])

        @pl.when(d > 0)
        def _():
            sent(N - 1 - p, fwd_sem.at[N - 1 - p])
    sent(slot_lo, fwd_sem.at[slot_lo])

    @pl.when(sib < c)
    def _():
        sent(slot_hi, fwd_sem.at[slot_hi])

    @pl.when(d > 0)
    def _():
        sent(slot_ca, fwd_sem.at[slot_ca])

    @pl.when(d < n_dp - 1)
    def _():
        sent(slot_hi, dp_sem.at[0])


def solution(mesh):
    n_ctx = mesh.shape["ctx"]
    n_dp = mesh.shape["dp"]
    freq = ROPE_BASE ** (-2.0 * np.arange(HD // 2, dtype=np.float64) / HD)
    freq = np.concatenate([freq, freq]).astype(np.float32)[None]

    def per_device(queries, keys, values, doc_start):
        tok = queries.shape[1]
        half = tok // 2
        groups = H // KVH
        np_half = max(n_ctx // 2 - 1, 1)
        hbm = pl.BlockSpec(memory_space=pl.ANY)
        return pl.pallas_call(
            functools.partial(kernel, n_ctx, n_dp),
            out_shape=jax.ShapeDtypeStruct(queries.shape, jnp.bfloat16),
            in_specs=[hbm] * 5,
            out_specs=pl.BlockSpec(memory_space=pl.ANY),
            scratch_shapes=[
                pltpu.VMEM((tok, H * HD), jnp.bfloat16),
                pltpu.VMEM((tok, KVH * HD), jnp.bfloat16),
                pltpu.VMEM((1, tok), jnp.int32),
                pltpu.VMEM((1, HD), jnp.float32),
                pltpu.VMEM((3 * n_ctx, half, 2 * KVH * HD), jnp.bfloat16),
                pltpu.VMEM((KVH, groups * tok, HD), jnp.bfloat16),
                pltpu.VMEM((tok, 3 * n_ctx * half), jnp.float32),
                pltpu.VMEM((KVH, groups * tok, HD), jnp.float32),
                pltpu.VMEM((KVH, groups * tok, 2 * HD), jnp.float32),
                pltpu.VMEM((KVH, tok, groups * HD), jnp.bfloat16),
                pltpu.SemaphoreType.DMA((6,)),
                pltpu.SemaphoreType.DMA((KVH,)),
                pltpu.SemaphoreType.DMA((3 * n_ctx,)),
                pltpu.SemaphoreType.DMA((3 * n_ctx,)),
                pltpu.SemaphoreType.DMA((np_half,)),
                pltpu.SemaphoreType.DMA((np_half,)),
                pltpu.SemaphoreType.DMA((np_half,)),
                pltpu.SemaphoreType.DMA((1 + np_half,)),
            ],
            compiler_params=pltpu.CompilerParams(
                collective_id=0, has_side_effects=True, vmem_limit_bytes=48 * 1024 * 1024
            ),
        )(*[pltpu.with_memory_space_constraint(x, pltpu.HBM) for x in (queries, keys, values, doc_start, jnp.asarray(freq))])

    return jax.shard_map(
        per_device,
        mesh=mesh,
        in_specs=(P("dp", "ctx", None), P("dp", "ctx", None), P("dp", "ctx", None), P("dp", "ctx")),
        out_specs=P("dp", "ctx", None),
        check_vma=False,
    )
```

```python
import functools
import math

import jax
import jax.numpy as jnp
import numpy as np
from jax import lax
from jax.experimental import pallas as pl
from jax.experimental.pallas import tpu as pltpu
from jax.sharding import PartitionSpec as P

H = 32
KVH = 4
HD = 128
ROPE_BASE = 500000.0
FILL = -1e30
class Parts:
    def __init__(self, copies):
        self.copies = copies

    def start(self):
        for copy in self.copies:
            copy.start()

    def wait_recv(self):
        for copy in self.copies:
            copy.wait_recv()

    def wait_send(self):
        for copy in self.copies:
            copy.wait_send()


MESH = pl.DeviceIdType.MESH
C2 = HD ** (-0.5) * math.log2(math.e)


def cos_sin(angles, want_cos):
    n = jnp.floor(angles * (2.0 / math.pi) + 0.5)
    r = ((angles - n * 1.5703125) - n * 4.837512969970703125e-4) - n * 7.54978995489188216e-8
    z = r * r
    s = ((-1.9515295891e-4 * z + 8.3321608736e-3) * z - 1.6666654611e-1) * z * r + r
    c = ((2.443315711809948e-5 * z - 1.388731625493765e-3) * z + 4.166664568298827e-2) * z * z - 0.5 * z + 1.0
    quadrant = n.astype(jnp.int32) + jnp.where(want_cos, 1, 0)
    v = jnp.where((quadrant & 1) == 1, c, s)
    return jnp.where((quadrant & 2) == 2, -v, v)


def kernel(n_ctx, n_dp, q_hbm, k_hbm, v_hbm, ds_hbm, freq_hbm, o_hbm,
           q_in, k_in, ds_in, freq_in, kv, q_rot, bias, m_st, acc, o_buf,
           in_sem, out_sem, recv_sem, fwd_sem, lo_sem, hi_sem, ca_sem, dp_sem):
    N = n_ctx
    d = lax.axis_index("dp")
    c = lax.axis_index("ctx")
    sib = c + 1 - 2 * (c % 2)
    half = q_in.shape[0] // 2
    feats = KVH * HD
    groups = H // KVH
    peers = [lax.rem(c + 2 * t, N) for t in range(1, N // 2)]
    slot_lo = N + c
    slot_hi = 3 * N - 1 - c
    slot_ca = N - 1 - c

    cp_ds = pltpu.make_async_copy(ds_hbm, ds_in, in_sem.at[0])
    cp_fr = pltpu.make_async_copy(freq_hbm, freq_in, in_sem.at[1])
    cp_k = pltpu.make_async_copy(k_hbm.at[0], k_in, in_sem.at[2])
    cp_v0 = pltpu.make_async_copy(v_hbm.at[0, pl.ds(0, half)], kv.at[slot_lo, :, pl.ds(feats, feats)], in_sem.at[3])
    cp_v1 = pltpu.make_async_copy(v_hbm.at[0, pl.ds(half, half)], kv.at[slot_hi, :, pl.ds(feats, feats)], in_sem.at[4])
    cp_q = pltpu.make_async_copy(q_hbm.at[0], q_in, in_sem.at[5])
    for cp in (cp_ds, cp_fr, cp_k, cp_v0, cp_v1, cp_q):
        cp.start()

    barrier = pltpu.get_barrier_semaphore()
    pl.semaphore_signal(barrier, inc=1, device_id=(d, sib), device_id_type=MESH)
    for p in peers:
        pl.semaphore_signal(barrier, inc=1, device_id=(d, p), device_id_type=MESH)

    @pl.when(d > 0)
    def _():
        pl.semaphore_signal(barrier, inc=1, device_id=(d - 1, c), device_id_type=MESH)

    cp_ds.wait()
    cp_fr.wait()
    tok = 2 * half
    starts = jnp.transpose(jnp.broadcast_to(ds_in[...].astype(jnp.float32), (HD, tok)))
    row = lax.broadcasted_iota(jnp.int32, (tok, HD), 0)
    lane = lax.broadcasted_iota(jnp.int32, (tok, HD), 1)
    pos = jnp.where(row < half, c * half + row, (2 * N - 2 - c) * half + row)
    posf = pos.astype(jnp.float32)
    low_lane = lane < HD // 2
    trig = cos_sin((posf - starts) * freq_in[...], low_lane)
    trig_r = pltpu.roll(trig, HD // 2, 1)
    cosine = jnp.where(low_lane, trig, trig_r)
    sine = jnp.where(low_lane, -trig_r, trig)

    cp_k.wait()
    for h in range(KVH):
        x = k_in[:, h * HD:(h + 1) * HD].astype(jnp.float32)
        y = (x * cosine + pltpu.roll(x, HD // 2, 1) * sine).astype(jnp.bfloat16)
        kv[slot_lo, :, h * HD:(h + 1) * HD] = y[:half]
        kv[slot_hi, :, h * HD:(h + 1) * HD] = y[half:]
    cp_v0.wait()
    cp_v1.wait()

    has_next = jnp.where(d < n_dp - 1, 1, 0)
    pl.semaphore_wait(barrier, N // 2 + has_next)

    part = half // 2

    def push(src_slot, dst_slot, send, dev, parts=(0, 1)):
        return Parts([pltpu.make_async_remote_copy(
            src_ref=kv.at[src_slot, pl.ds(i * part, part)], dst_ref=kv.at[dst_slot, pl.ds(i * part, part)],
            send_sem=send.at[i], recv_sem=recv_sem.at[dst_slot, i], device_id=dev, device_id_type=MESH)
            for i in parts])

    def got(slot, parts=(0, 1)):
        push(slot, slot, fwd_sem.at[slot], (d, sib), parts).wait_recv()

    def forward(slot, parts=(0, 1)):
        push(slot, slot, fwd_sem.at[slot], (d, sib), parts).start()

    to_dp = push(slot_hi, slot_ca, dp_sem.at[0], (d + 1, c))

    @pl.when(d < n_dp - 1)
    def _():
        to_dp.start()

    for t, p in enumerate(peers):
        @pl.when(p < c)
        def _():
            push(slot_hi, slot_hi, hi_sem.at[t], (d, p)).start()

    for t, p in enumerate(peers):
        push(slot_lo, slot_lo, lo_sem.at[t], (d, p)).start()

    forward(slot_lo)

    @pl.when(sib < c)
    def _():
        forward(slot_hi)

    def clear(slot):
        kv[slot] = jnp.zeros(kv.shape[1:], kv.dtype)

    for s in range(2 * N, 3 * N):
        @pl.when(s > slot_hi)
        def _():
            clear(s)

    @pl.when(d == 0)
    def _():
        for s in range(N):
            clear(s)

    for s in range(0, 3 * N * half, 128):
        key = (lane + (s - N * half)).astype(jnp.float32)
        bias[:, s:s + 128] = jnp.where((key <= posf) & (key >= starts), 0.0, FILL)

    cp_q.wait()
    for h in range(H):
        x = q_in[:, h * HD:(h + 1) * HD].astype(jnp.float32)
        y = (x * cosine + pltpu.roll(x, HD // 2, 1) * sine).astype(jnp.bfloat16)
        g = h % groups
        q_rot[h // groups, g * half:(g + 1) * half] = y[:half]
        q_rot[h // groups, (groups + g) * half:(groups + g + 1) * half] = y[half:]

    for i in range(2):
        @pl.when(d > 0)
        def _():
            got(slot_ca, (i,))
            for t, p in enumerate(peers):
                @pl.when(p > c)
                def _():
                    push(slot_ca, slot_ca, ca_sem.at[t], (d, p), (i,)).start()
            forward(slot_ca, (i,))

        for t, p in enumerate(peers):
            @pl.when(p > c)
            def _():
                got(3 * N - 1 - p, (i,))

                @pl.when(d < n_dp - 1)
                def _():
                    push(3 * N - 1 - p, N - 1 - p, dp_sem.at[1 + t], (d + 1, c), (i,)).start()

                forward(3 * N - 1 - p, (i,))

    for p in peers:
        got(N + p)
        forward(N + p)
    got(N + sib)
    for p in peers:
        got(N + p + 1 - 2 * (p % 2))

    rows = groups * half
    ones = jnp.ones((N * half, HD), jnp.bfloat16)

    def piece(kvh, which, base, first):
        col = pl.multiple_of(kvh * HD, HD)
        vcol = pl.multiple_of(feats + kvh * HD, HD)
        k = kv[base:base + N, :, pl.ds(col, HD)].reshape(N * half, HD)
        v = kv[base:base + N, :, pl.ds(vcol, HD)].reshape(N * half, HD)
        va = jnp.concatenate([v, ones], axis=1)
        for w in which:
            r0 = w * rows
            q = q_rot[kvh, r0:r0 + rows]
            s = lax.dot_general(q, k, (((1,), (1,)), ((), ())), preferred_element_type=jnp.float32)
            b = bias[w * half:(w + 1) * half, base * half:(base + N) * half]
            s = s.reshape(groups, half, N * half) * C2 + b[None]
            top = jnp.max(s, axis=-1, keepdims=True).reshape(rows, 1)
            if not first:
                old = m_st[kvh, r0:r0 + rows]
                new = jnp.maximum(old, top)
                scale = jnp.exp2(old - new)
                top = new[:, :1]
            else:
                new = jnp.broadcast_to(top, (rows, HD))
            m_st[kvh, r0:r0 + rows] = new
            wide = jnp.concatenate([new] * (N * half // HD), axis=1)
            w_bf = jnp.exp2(s.reshape(rows, N * half) - wide).astype(jnp.bfloat16)
            pv = jnp.dot(w_bf, va, preferred_element_type=jnp.float32)
            if not first:
                pv = pv + acc[kvh, r0:r0 + rows] * jnp.concatenate([scale, scale], axis=1)
            acc[kvh, r0:r0 + rows] = pv

    def low(kvh, _):
        piece(kvh, (0, 1), N, True)
        return _

    def high(kvh, _):
        piece(kvh, (1,), 2 * N, False)
        return _

    lax.fori_loop(0, KVH, low, 0, unroll=True)

    @pl.when(d > 0)
    def _():
        for p in peers:
            got(N - 1 - p)
            forward(N - 1 - p)

    @pl.when(sib > c)
    def _():
        got(3 * N - 1 - sib)
    for p in peers:
        @pl.when(p > c)
        def _():
            got(3 * N - 1 - (p + 1 - 2 * (p % 2)))

    lax.fori_loop(0, KVH, high, 0, unroll=True)

    @pl.when(d > 0)
    def _():
        got(N - 1 - sib)
        for p in peers:
            got(N - 1 - (p + 1 - 2 * (p % 2)))

    def carried(kvh, _):
        piece(kvh, (0, 1), 0, False)
        for w in range(2):
            for g in range(groups):
                r0 = w * rows + g * half
                a = acc[kvh, r0:r0 + half]
                o = (a[:, :HD] / a[:, HD:]).astype(jnp.bfloat16)
                o_buf[kvh, w * half:(w + 1) * half, g * HD:(g + 1) * HD] = o
        pltpu.make_async_copy(o_buf.at[kvh], o_hbm.at[0, :, pl.ds(pl.multiple_of(kvh * groups * HD, HD), groups * HD)], out_sem.at[kvh]).start()
        return _

    lax.fori_loop(0, KVH, carried, 0, unroll=True)

    for kvh in range(KVH):
        pltpu.make_async_copy(o_buf.at[kvh], o_hbm.at[0, :, pl.ds(kvh * groups * HD, groups * HD)], out_sem.at[kvh]).wait()

    def sent(slot, sem):
        push(slot, slot, sem, (d, sib)).wait_send()

    for t, p in enumerate(peers):
        sent(slot_lo, lo_sem.at[t])
        sent(N + p, fwd_sem.at[N + p])

        @pl.when(p < c)
        def _():
            sent(slot_hi, hi_sem.at[t])

        @pl.when(p > c)
        def _():
            sent(3 * N - 1 - p, fwd_sem.at[3 * N - 1 - p])

            @pl.when(d < n_dp - 1)
            def _():
                sent(3 * N - 1 - p, dp_sem.at[1 + t])

            @pl.when(d > 0)
            def _():
                sent(slot_ca, ca_sem.at[t])

        @pl.when(d > 0)
        def _():
            sent(N - 1 - p, fwd_sem.at[N - 1 - p])
    sent(slot_lo, fwd_sem.at[slot_lo])

    @pl.when(sib < c)
    def _():
        sent(slot_hi, fwd_sem.at[slot_hi])

    @pl.when(d > 0)
    def _():
        sent(slot_ca, fwd_sem.at[slot_ca])

    @pl.when(d < n_dp - 1)
    def _():
        sent(slot_hi, dp_sem.at[0])


def solution(mesh):
    n_ctx = mesh.shape["ctx"]
    n_dp = mesh.shape["dp"]
    freq = ROPE_BASE ** (-2.0 * np.arange(HD // 2, dtype=np.float64) / HD)
    freq = np.concatenate([freq, freq]).astype(np.float32)[None]

    def per_device(queries, keys, values, doc_start):
        tok = queries.shape[1]
        half = tok // 2
        groups = H // KVH
        np_half = max(n_ctx // 2 - 1, 1)
        hbm = pl.BlockSpec(memory_space=pl.ANY)
        return pl.pallas_call(
            functools.partial(kernel, n_ctx, n_dp),
            out_shape=jax.ShapeDtypeStruct(queries.shape, jnp.bfloat16),
            in_specs=[hbm] * 5,
            out_specs=pl.BlockSpec(memory_space=pl.ANY),
            scratch_shapes=[
                pltpu.VMEM((tok, H * HD), jnp.bfloat16),
                pltpu.VMEM((tok, KVH * HD), jnp.bfloat16),
                pltpu.VMEM((1, tok), jnp.int32),
                pltpu.VMEM((1, HD), jnp.float32),
                pltpu.VMEM((3 * n_ctx, half, 2 * KVH * HD), jnp.bfloat16),
                pltpu.VMEM((KVH, groups * tok, HD), jnp.bfloat16),
                pltpu.VMEM((tok, 3 * n_ctx * half), jnp.float32),
                pltpu.VMEM((KVH, groups * tok, HD), jnp.float32),
                pltpu.VMEM((KVH, groups * tok, 2 * HD), jnp.float32),
                pltpu.VMEM((KVH, tok, groups * HD), jnp.bfloat16),
                pltpu.SemaphoreType.DMA((6,)),
                pltpu.SemaphoreType.DMA((KVH,)),
                pltpu.SemaphoreType.DMA((3 * n_ctx, 2)),
                pltpu.SemaphoreType.DMA((3 * n_ctx, 2)),
                pltpu.SemaphoreType.DMA((np_half, 2)),
                pltpu.SemaphoreType.DMA((np_half, 2)),
                pltpu.SemaphoreType.DMA((np_half, 2)),
                pltpu.SemaphoreType.DMA((1 + np_half, 2)),
            ],
            compiler_params=pltpu.CompilerParams(
                collective_id=0, has_side_effects=True, vmem_limit_bytes=48 * 1024 * 1024
            ),
        )(*[pltpu.with_memory_space_constraint(x, pltpu.HBM) for x in (queries, keys, values, doc_start, jnp.asarray(freq))])

    return jax.shard_map(
        per_device,
        mesh=mesh,
        in_specs=(P("dp", "ctx", None), P("dp", "ctx", None), P("dp", "ctx", None), P("dp", "ctx")),
        out_specs=P("dp", "ctx", None),
        check_vma=False,
    )
```

```python
import functools
import math

import jax
import jax.numpy as jnp
import numpy as np
from jax import lax
from jax.experimental import pallas as pl
from jax.experimental.pallas import tpu as pltpu
from jax.sharding import PartitionSpec as P

H = 32
KVH = 4
HD = 128
ROPE_BASE = 500000.0
FILL = -1e30
MESH = pl.DeviceIdType.MESH
C2 = HD ** (-0.5) * math.log2(math.e)


def cos_sin(angles, want_cos):
    n = jnp.floor(angles * (2.0 / math.pi) + 0.5)
    r = ((angles - n * 1.5703125) - n * 4.837512969970703125e-4) - n * 7.54978995489188216e-8
    z = r * r
    s = ((-1.9515295891e-4 * z + 8.3321608736e-3) * z - 1.6666654611e-1) * z * r + r
    c = ((2.443315711809948e-5 * z - 1.388731625493765e-3) * z + 4.166664568298827e-2) * z * z - 0.5 * z + 1.0
    quadrant = n.astype(jnp.int32) + jnp.where(want_cos, 1, 0)
    v = jnp.where((quadrant & 1) == 1, c, s)
    return jnp.where((quadrant & 2) == 2, -v, v)


def kernel(n_ctx, n_dp, q_hbm, k_hbm, v_hbm, ds_hbm, freq_hbm, o_hbm,
           q_in, k_in, ds_in, freq_in, kv, q_rot, bias, m_st, acc, o_buf,
           in_sem, out_sem, recv_sem, fwd_sem, lo_sem, hi_sem, ca_sem, dp_sem):
    N = n_ctx
    d = lax.axis_index("dp")
    c = lax.axis_index("ctx")
    sib = c + 1 - 2 * (c % 2)
    half = q_in.shape[0] // 2
    feats = KVH * HD
    groups = H // KVH
    peers = [lax.rem(c + 2 * t, N) for t in range(1, N // 2)]
    slot_lo = N + c
    slot_hi = 3 * N - 1 - c
    slot_ca = N - 1 - c

    cp_ds = pltpu.make_async_copy(ds_hbm, ds_in, in_sem.at[0])
    cp_fr = pltpu.make_async_copy(freq_hbm, freq_in, in_sem.at[1])
    cp_k = pltpu.make_async_copy(k_hbm.at[0], k_in, in_sem.at[2])
    cp_v0 = pltpu.make_async_copy(v_hbm.at[0, pl.ds(0, half)], kv.at[slot_lo, :, pl.ds(feats, feats)], in_sem.at[3])
    cp_v1 = pltpu.make_async_copy(v_hbm.at[0, pl.ds(half, half)], kv.at[slot_hi, :, pl.ds(feats, feats)], in_sem.at[4])
    cp_q = pltpu.make_async_copy(q_hbm.at[0], q_in, in_sem.at[5])
    for cp in (cp_ds, cp_fr, cp_k, cp_v0, cp_v1, cp_q):
        cp.start()

    barrier = pltpu.get_barrier_semaphore()
    pl.semaphore_signal(barrier, inc=1, device_id=(d, sib), device_id_type=MESH)
    for p in peers:
        pl.semaphore_signal(barrier, inc=1, device_id=(d, p), device_id_type=MESH)

    @pl.when(d > 0)
    def _():
        pl.semaphore_signal(barrier, inc=1, device_id=(d - 1, c), device_id_type=MESH)

    cp_ds.wait()
    cp_fr.wait()
    tok = 2 * half
    starts = jnp.transpose(jnp.broadcast_to(ds_in[...].astype(jnp.float32), (HD, tok)))
    row = lax.broadcasted_iota(jnp.int32, (tok, HD), 0)
    lane = lax.broadcasted_iota(jnp.int32, (tok, HD), 1)
    pos = jnp.where(row < half, c * half + row, (2 * N - 2 - c) * half + row)
    posf = pos.astype(jnp.float32)
    low_lane = lane < HD // 2
    trig = cos_sin((posf - starts) * freq_in[...], low_lane)
    trig_r = pltpu.roll(trig, HD // 2, 1)
    cosine = jnp.where(low_lane, trig, trig_r)
    sine = jnp.where(low_lane, -trig_r, trig)

    cp_k.wait()
    for h in range(KVH):
        x = k_in[:, h * HD:(h + 1) * HD].astype(jnp.float32)
        y = (x * cosine + pltpu.roll(x, HD // 2, 1) * sine).astype(jnp.bfloat16)
        kv[slot_lo, :, h * HD:(h + 1) * HD] = y[:half]
        kv[slot_hi, :, h * HD:(h + 1) * HD] = y[half:]
    cp_v0.wait()
    cp_v1.wait()

    has_next = jnp.where(d < n_dp - 1, 1, 0)
    pl.semaphore_wait(barrier, N // 2 + has_next)

    def push(src_slot, dst_slot, send, dev):
        return pltpu.make_async_remote_copy(
            src_ref=kv.at[src_slot], dst_ref=kv.at[dst_slot], send_sem=send,
            recv_sem=recv_sem.at[dst_slot], device_id=dev, device_id_type=MESH)

    def got(slot):
        push(slot, slot, fwd_sem.at[slot], (d, sib)).wait_recv()

    def forward(slot):
        push(slot, slot, fwd_sem.at[slot], (d, sib)).start()

    to_dp = push(slot_hi, slot_ca, dp_sem.at[0], (d + 1, c))

    @pl.when(d < n_dp - 1)
    def _():
        to_dp.start()

    for t, p in enumerate(peers):
        @pl.when(p < c)
        def _():
            push(slot_hi, slot_hi, hi_sem.at[t], (d, p)).start()

    for t, p in enumerate(peers):
        push(slot_lo, slot_lo, lo_sem.at[t], (d, p)).start()

    forward(slot_lo)

    @pl.when(sib < c)
    def _():
        forward(slot_hi)

    def clear(slot):
        kv[slot] = jnp.zeros(kv.shape[1:], kv.dtype)

    for s in range(2 * N, 3 * N):
        @pl.when(s > slot_hi)
        def _():
            clear(s)

    @pl.when(d == 0)
    def _():
        for s in range(N):
            clear(s)

    for s in range(0, 3 * N * half, 128):
        key = (lane + (s - N * half)).astype(jnp.float32)
        bias[:, s:s + 128] = jnp.where((key <= posf) & (key >= starts), 0.0, FILL)

    cp_q.wait()
    for h in range(H):
        x = q_in[:, h * HD:(h + 1) * HD].astype(jnp.float32)
        y = (x * cosine + pltpu.roll(x, HD // 2, 1) * sine).astype(jnp.bfloat16)
        g = h % groups
        q_rot[h // groups, g * half:(g + 1) * half] = y[:half]
        q_rot[h // groups, (groups + g) * half:(groups + g + 1) * half] = y[half:]

    @pl.when(d > 0)
    def _():
        got(slot_ca)
        for t, p in enumerate(peers):
            @pl.when(p > c)
            def _():
                push(slot_ca, slot_ca, ca_sem.at[t], (d, p)).start()
        forward(slot_ca)

    for t, p in enumerate(peers):
        @pl.when(p > c)
        def _():
            got(3 * N - 1 - p)
            forward(3 * N - 1 - p)

            @pl.when(d < n_dp - 1)
            def _():
                push(3 * N - 1 - p, N - 1 - p, dp_sem.at[1 + t], (d + 1, c)).start()

    for p in peers:
        got(N + p)
        forward(N + p)
    got(N + sib)
    for p in peers:
        got(N + p + 1 - 2 * (p % 2))

    rows = groups * half
    ones = jnp.ones((N * half, HD), jnp.bfloat16)

    def piece(kvh, which, base, first):
        col = pl.multiple_of(kvh * HD, HD)
        vcol = pl.multiple_of(feats + kvh * HD, HD)
        k = kv[base:base + N, :, pl.ds(col, HD)].reshape(N * half, HD)
        v = kv[base:base + N, :, pl.ds(vcol, HD)].reshape(N * half, HD)
        va = jnp.concatenate([v, ones], axis=1)
        for w in which:
            r0 = w * rows
            q = q_rot[kvh, r0:r0 + rows]
            s = lax.dot_general(q, k, (((1,), (1,)), ((), ())), preferred_element_type=jnp.float32)
            b = bias[w * half:(w + 1) * half, base * half:(base + N) * half]
            s = s.reshape(groups, half, N * half) * C2 + b[None]
            top = jnp.max(s, axis=-1, keepdims=True).reshape(rows, 1)
            if not first:
                old = m_st[kvh, r0:r0 + rows]
                new = jnp.maximum(old, top)
                scale = jnp.exp2(old - new)
                top = new[:, :1]
            else:
                new = jnp.broadcast_to(top, (rows, HD))
            m_st[kvh, r0:r0 + rows] = new
            wide = jnp.concatenate([new] * (N * half // HD), axis=1)
            w_bf = jnp.exp2(s.reshape(rows, N * half) - wide).astype(jnp.bfloat16)
            pv = jnp.dot(w_bf, va, preferred_element_type=jnp.float32)
            if not first:
                pv = pv + acc[kvh, r0:r0 + rows] * jnp.concatenate([scale, scale], axis=1)
            acc[kvh, r0:r0 + rows] = pv

    def low(kvh, _):
        piece(kvh, (0, 1), N, True)
        return _

    def high(kvh, _):
        piece(kvh, (1,), 2 * N, False)
        return _

    lax.fori_loop(0, KVH, low, 0, unroll=True)

    @pl.when(d > 0)
    def _():
        for p in peers:
            got(N - 1 - p)
            forward(N - 1 - p)

    @pl.when(sib > c)
    def _():
        got(3 * N - 1 - sib)
    for p in peers:
        @pl.when(p > c)
        def _():
            got(3 * N - 1 - (p + 1 - 2 * (p % 2)))

    lax.fori_loop(0, KVH, high, 0, unroll=True)

    @pl.when(d > 0)
    def _():
        got(N - 1 - sib)
        for p in peers:
            got(N - 1 - (p + 1 - 2 * (p % 2)))

    def carried(kvh, _):
        piece(kvh, (0, 1), 0, False)
        for w in range(2):
            for g in range(groups):
                r0 = w * rows + g * half
                a = acc[kvh, r0:r0 + half]
                o = (a[:, :HD] / a[:, HD:]).astype(jnp.bfloat16)
                o_buf[kvh, w * half:(w + 1) * half, g * HD:(g + 1) * HD] = o
        pltpu.make_async_copy(o_buf.at[kvh], o_hbm.at[0, :, pl.ds(pl.multiple_of(kvh * groups * HD, HD), groups * HD)], out_sem.at[kvh]).start()
        return _

    lax.fori_loop(0, KVH, carried, 0, unroll=True)

    for kvh in range(KVH):
        pltpu.make_async_copy(o_buf.at[kvh], o_hbm.at[0, :, pl.ds(kvh * groups * HD, groups * HD)], out_sem.at[kvh]).wait()

    def sent(slot, sem):
        push(slot, slot, sem, (d, sib)).wait_send()

    for t, p in enumerate(peers):
        sent(slot_lo, lo_sem.at[t])
        sent(N + p, fwd_sem.at[N + p])

        @pl.when(p < c)
        def _():
            sent(slot_hi, hi_sem.at[t])

        @pl.when(p > c)
        def _():
            sent(3 * N - 1 - p, fwd_sem.at[3 * N - 1 - p])

            @pl.when(d < n_dp - 1)
            def _():
                sent(3 * N - 1 - p, dp_sem.at[1 + t])

            @pl.when(d > 0)
            def _():
                sent(slot_ca, ca_sem.at[t])

        @pl.when(d > 0)
        def _():
            sent(N - 1 - p, fwd_sem.at[N - 1 - p])
    sent(slot_lo, fwd_sem.at[slot_lo])

    @pl.when(sib < c)
    def _():
        sent(slot_hi, fwd_sem.at[slot_hi])

    @pl.when(d > 0)
    def _():
        sent(slot_ca, fwd_sem.at[slot_ca])

    @pl.when(d < n_dp - 1)
    def _():
        sent(slot_hi, dp_sem.at[0])


def solution(mesh):
    n_ctx = mesh.shape["ctx"]
    n_dp = mesh.shape["dp"]
    freq = ROPE_BASE ** (-2.0 * np.arange(HD // 2, dtype=np.float64) / HD)
    freq = np.concatenate([freq, freq]).astype(np.float32)[None]

    def per_device(queries, keys, values, doc_start):
        tok = queries.shape[1]
        half = tok // 2
        groups = H // KVH
        np_half = max(n_ctx // 2 - 1, 1)
        hbm = pl.BlockSpec(memory_space=pl.ANY)
        return pl.pallas_call(
            functools.partial(kernel, n_ctx, n_dp),
            out_shape=jax.ShapeDtypeStruct(queries.shape, jnp.bfloat16),
            in_specs=[hbm] * 5,
            out_specs=pl.BlockSpec(memory_space=pl.ANY),
            scratch_shapes=[
                pltpu.VMEM((tok, H * HD), jnp.bfloat16),
                pltpu.VMEM((tok, KVH * HD), jnp.bfloat16),
                pltpu.VMEM((1, tok), jnp.int32),
                pltpu.VMEM((1, HD), jnp.float32),
                pltpu.VMEM((3 * n_ctx, half, 2 * KVH * HD), jnp.bfloat16),
                pltpu.VMEM((KVH, groups * tok, HD), jnp.bfloat16),
                pltpu.VMEM((tok, 3 * n_ctx * half), jnp.float32),
                pltpu.VMEM((KVH, groups * tok, HD), jnp.float32),
                pltpu.VMEM((KVH, groups * tok, 2 * HD), jnp.float32),
                pltpu.VMEM((KVH, tok, groups * HD), jnp.bfloat16),
                pltpu.SemaphoreType.DMA((6,)),
                pltpu.SemaphoreType.DMA((KVH,)),
                pltpu.SemaphoreType.DMA((3 * n_ctx,)),
                pltpu.SemaphoreType.DMA((3 * n_ctx,)),
                pltpu.SemaphoreType.DMA((np_half,)),
                pltpu.SemaphoreType.DMA((np_half,)),
                pltpu.SemaphoreType.DMA((np_half,)),
                pltpu.SemaphoreType.DMA((1 + np_half,)),
            ],
            compiler_params=pltpu.CompilerParams(
                collective_id=0, has_side_effects=True, vmem_limit_bytes=48 * 1024 * 1024
            ),
        )(*[pltpu.with_memory_space_constraint(x, pltpu.HBM) for x in (queries, keys, values, doc_start, jnp.asarray(freq))])

    return jax.shard_map(
        per_device,
        mesh=mesh,
        in_specs=(P("dp", "ctx", None), P("dp", "ctx", None), P("dp", "ctx", None), P("dp", "ctx")),
        out_specs=P("dp", "ctx", None),
        check_vma=False,
    )
```
